512 devices in a mesh: rep: 64 (over z, y_hi, core), fsdp: 8 (over y_lo, x).
Axes of the slice: x: 4, y: 4 (y_hi: 2, y_lo: 2; y = y_hi * 2 + y_lo), z: 16, core: 2. Of those that a mesh axis runs over, the one named last changes fastest.
Arguments:
- anchor: float32 [256, 4096], P('fsdp'), may hold values from -3 to 3
- inner_weights: bfloat16 [64, 256, 4096], P('rep', 'fsdp'), may hold values from -300 to 300
- momentum: float32 [256, 4096], P('fsdp'), may hold values from -1.5 to 1.5
- adam_first: float32 [64, 256, 4096], P('rep', 'fsdp'), may hold values from -1.5 to 1.5
- adam_second: float32 [64, 256, 4096], P('rep', 'fsdp'), may hold values from 0.01 to 1
Outputs:
- new_anchor: float32 [256, 4096], P('fsdp')
- new_momentum: float32 [256, 4096], P('fsdp')
- new_inner: bfloat16 [64, 256, 4096], P('rep', 'fsdp')
- new_first: float32 [64, 256, 4096], P('rep', 'fsdp')
- new_second: float32 [64, 256, 4096], P('rep', 'fsdp')
The draws below stay inside these ranges and needn't reach their ends.
All inputs are finite; a program needn't handle non-finite values.
Results may differ from the reference program's by a relative error of at most 0.012.
Values sent between devices are 32-bit elements; how exact they have to be, the bound alone decides.
No kernel may reach another device: no remote copies, remote signals or barrier semaphores. Data moves between devices by JAX's collectives and lax.ppermute only.
A program may use at most 64 MiB of HBM per device.

```python
import math
import jax
import jax.numpy as jnp
from jax import lax

D = 4096
ROWS = 256
REPLICAS = 64


def anchor_values(key):
    base_key = jax.random.fold_in(key, 11)
    return 0.5 * jnp.clip(jax.random.normal(base_key, (ROWS, D), jnp.float32), -6.0, 6.0)


def draw_anchor(key, part):
    return anchor_values(key)


def draw_inner_weights(key, part):
    shared = anchor_values(key)
    key = jax.random.fold_in(key, 3)
    row_key, col_key, own_key = jax.random.split(key, 3)
    rise_total = 3.0
    divisor = 20.0
    row_index = jnp.arange(ROWS).astype(jnp.float32) / ROWS
    row_scale = jnp.exp(jax.random.uniform(row_key, (ROWS,), jnp.float32) * math.log(10.0)) * jnp.exp(math.log(rise_total) * row_index)
    col_scale = jnp.exp(jax.random.uniform(col_key, (D,), jnp.float32) * math.log(10.0))
    scales = row_scale[:, None] * col_scale[None, :] / divisor
    own_part = jnp.clip(jax.random.normal(own_key, (REPLICAS, ROWS, D), jnp.float32), -5.0, 5.0)
    drift = scales[None] * own_part
    return (shared[None] - drift).astype(jnp.bfloat16)


def block_levels(key, extent, cuts, smallest, largest):
    factor_of, own = 1.0, jax.random.fold_in(key, 6)
    for axis_at, blocks in cuts:
        draws = jnp.exp(jax.random.uniform(jax.random.fold_in(own, axis_at), (blocks,), jnp.float32, smallest / len(cuts), largest / len(cuts)))
        factor_of = factor_of * jnp.repeat(draws, extent[axis_at] // blocks).reshape([-1 if axis == axis_at else 1 for axis in range(len(extent))])
    return factor_of


def normal_values(stream_key, dims, deviation, reach, shards=(), dtype=jnp.bfloat16):
    loudness = block_levels(stream_key, dims, shards, -0.22, 0.18) if shards else 1.0
    drawn = jax.random.normal(stream_key, dims, jnp.float32) * deviation * loudness
    return jnp.minimum(jnp.maximum(drawn, -reach), reach).astype(dtype)


def setup_inputs(seed: int = 0) -> dict:
    arg_keys = jax.random.split(jax.random.key(seed), 6)
    return {
        "anchor": draw_anchor(jax.random.fold_in(arg_keys[5], 71), 0),
        "inner_weights": draw_inner_weights(jax.random.fold_in(arg_keys[5], 71), 0),
        "momentum": normal_values(arg_keys[2], (ROWS, D), 0.1, 1.5, ((0, 8),), jnp.float32),
        "adam_first": normal_values(arg_keys[3], (REPLICAS, ROWS, D), 0.1, 1.5, ((0, 64), (1, 8)), jnp.float32),
        "adam_second": jnp.clip(jnp.exp(math.log(1.0) - 4.6051702 * jax.random.uniform(arg_keys[4], (REPLICAS, ROWS, D), jnp.float32) ** block_levels(arg_keys[4], (REPLICAS, ROWS, D), ((0, 64), (1, 8)), -0.2, 0.2)), 0.01, 1.0),
    }


OUTER_MOMENTUM = 0.9
OUTER_RATE = 0.7
MIX_KEEP = 0.5
CLIP_RMS = 0.1
EPSILON = 1e-06

def reference(anchor, inner_weights, momentum, adam_first, adam_second):
    pseudo_grad = (anchor[None] - inner_weights.astype(jnp.float32)).astype(jnp.bfloat16)
    outer_grad = lax.optimization_barrier(jnp.sum(pseudo_grad.astype(jnp.float32), axis=0)) / REPLICAS
    mean_square = jnp.mean(outer_grad * outer_grad)
    clip_factor = jnp.minimum(1.0, CLIP_RMS / jnp.sqrt(mean_square + EPSILON))
    clipped = clip_factor * outer_grad
    new_momentum = OUTER_MOMENTUM * momentum + clipped
    new_anchor = anchor - OUTER_RATE * (clipped + OUTER_MOMENTUM * new_momentum)
    new_inner = (MIX_KEEP * inner_weights.astype(jnp.float32) + (1.0 - MIX_KEEP) * new_anchor[None]).astype(jnp.bfloat16)
    first_mean = lax.optimization_barrier(jnp.sum(adam_first, axis=0)) / REPLICAS
    second_mean = lax.optimization_barrier(jnp.sum(adam_second, axis=0)) / REPLICAS
    new_first = MIX_KEEP * adam_first + (1.0 - MIX_KEEP) * first_mean[None]
    new_second = MIX_KEEP * adam_second + (1.0 - MIX_KEEP) * second_mean[None]
    return (new_anchor, new_momentum, new_inner, new_first, new_second)
```

```python
import jax
import jax.numpy as jnp
from jax import lax
from jax.sharding import Mesh, PartitionSpec as P

OUTER_MOMENTUM = 0.9
OUTER_RATE = 0.7
MIX_KEEP = 0.5
CLIP_RMS = 0.1
EPSILON = 1e-06

AXES = ("z", "yh", "c", "yl", "x")
SIZES = (16, 2, 2, 2, 4)
REP = ("z", "yh", "c")
FSDP = ("yl", "x")
N_Z, N_Y, N_C = SIZES[:3]


def scatter_sum(parts, axis):
    return jnp.sum(lax.all_to_all(parts, axis, 0, 0), axis=0)


def gather_parts(part, axis):
    return lax.all_gather(part, axis, axis=0)


def per_device(anchor, inner_weights, momentum, adam_first, adam_second):
    rows, columns = anchor.shape
    replica_count = N_Z * N_Y * N_C
    entries_total = rows * columns * SIZES[3] * SIZES[4]
    inner_float = inner_weights[0].astype(jnp.float32)
    pseudo_grad = (anchor - inner_float).astype(jnp.bfloat16).astype(jnp.float32)
    own_rows = rows // (N_C * N_Y)

    def split(array):
        return array.reshape(N_C, N_Y, own_rows, columns)

    terms = jnp.stack([split(pseudo_grad), split(adam_first[0]), split(adam_second[0])], axis=2)
    terms = scatter_sum(terms, "c")
    terms = scatter_sum(terms, "yh")
    width = columns // N_Z
    terms = terms.reshape(3, own_rows, N_Z, width).transpose(2, 0, 1, 3)
    total = scatter_sum(terms, "z")
    mean = total / replica_count

    spread = lax.all_to_all(jnp.broadcast_to(mean[None], (N_Z,) + mean.shape), "z", 0, 0)
    spread = spread.transpose(1, 2, 0, 3).reshape(3, own_rows, columns)
    spread = gather_parts(spread, "yh")

    def whole(at):
        return gather_parts(spread[:, at], "c").reshape(rows, columns)

    outer_grad, first_mean, second_mean = whole(0), whole(1), whole(2)
    local_sum = jnp.sum(outer_grad * outer_grad)
    sums = lax.all_to_all(jnp.full((SIZES[3] * SIZES[4], 8, 128), local_sum), FSDP, 0, 0)
    mean_square = jnp.sum(sums[:, 0, 0]) / entries_total
    clip_factor = jnp.minimum(1.0, CLIP_RMS / jnp.sqrt(mean_square + EPSILON))
    clipped = clip_factor * outer_grad
    new_momentum = OUTER_MOMENTUM * momentum + clipped
    new_anchor = anchor - OUTER_RATE * (clipped + OUTER_MOMENTUM * new_momentum)
    new_inner = (MIX_KEEP * inner_float + (1.0 - MIX_KEEP) * new_anchor).astype(jnp.bfloat16)
    new_first = MIX_KEEP * adam_first[0] + (1.0 - MIX_KEEP) * first_mean
    new_second = MIX_KEEP * adam_second[0] + (1.0 - MIX_KEEP) * second_mean
    return (new_anchor, new_momentum, new_inner[None], new_first[None], new_second[None])


def solution(mesh):
    fine = Mesh(mesh.devices.reshape(SIZES), AXES)
    shared, own = P(FSDP, None), P(REP, FSDP, None)
    return jax.shard_map(
        per_device,
        mesh=fine,
        in_specs=(shared, own, shared, own, own),
        out_specs=(shared, shared, own, own, own),
        check_vma=False,
    )
```

```python
import jax
import jax.numpy as jnp
from jax import lax
from jax.sharding import Mesh, PartitionSpec as P

OUTER_MOMENTUM = 0.9
OUTER_RATE = 0.7
MIX_KEEP = 0.5
CLIP_RMS = 0.1
EPSILON = 1e-06

AXES = ("zs", "z1", "yh", "c", "yl", "x")
SIZES = (8, 2, 2, 2, 2, 4)
N_ZS, N_Z1, N_YH, N_C, N_YL, N_X = SIZES
REP = ("zs", "z1", "yh", "c")
NEAR = ("yh", "z1")
FSDP = ("yl", "x")
SWAP = ((0, 1), (1, 0))


def scatter_sum(parts, axis):
    return jnp.sum(lax.all_to_all(parts, axis, 0, 0), axis=0)


def gather_parts(part, axis, count):
    return lax.all_to_all(jnp.broadcast_to(part[None], (count,) + part.shape), axis, 0, 0)


def per_device(anchor, inner_weights, momentum, adam_first, adam_second):
    rows, columns = anchor.shape
    replica_count = N_ZS * N_Z1 * N_YH * N_C
    entries_total = rows * columns * N_YL * N_X
    inner_float = inner_weights[0].astype(jnp.float32)
    pseudo_grad = (anchor - inner_float).astype(jnp.bfloat16).astype(jnp.float32)
    block = (rows // (N_C * N_YH), columns // (N_Z1 * N_ZS))

    def split(array):
        array = array.reshape(N_C, N_YH, block[0], N_Z1 * N_ZS, block[1])
        return array.transpose(0, 1, 3, 2, 4).reshape((N_C, N_YH * N_Z1, N_ZS) + block)

    def join(blocks):
        blocks = blocks.reshape((N_C, N_YH, N_Z1 * N_ZS) + block)
        return blocks.transpose(0, 1, 3, 2, 4).reshape(rows, columns)

    terms = jnp.stack([split(pseudo_grad), split(adam_first[0]), split(adam_second[0])], axis=3)
    terms = scatter_sum(terms, "c")
    terms = scatter_sum(terms, NEAR)
    mean = scatter_sum(terms, "zs") / replica_count

    spread = gather_parts(mean, "zs", N_ZS)
    half = gather_parts(spread, NEAR, N_YH * N_Z1)
    other = lax.ppermute(half, "c", SWAP)

    own_grad = half[:, :, 0]
    squares = jnp.sum((own_grad * own_grad).reshape(-1, 8, 128), axis=0)
    groups = N_C * N_YL * N_X
    sums = lax.all_to_all(jnp.broadcast_to(squares[None], (groups, 8, 128)), ("c",) + FSDP, 0, 0)
    mean_square = jnp.sum(sums) / entries_total

    first_half = lax.axis_index("c") == 0
    both = jnp.stack([jnp.where(first_half, half, other), jnp.where(first_half, other, half)])
    outer_grad, first_mean, second_mean = (join(both[:, :, :, at]) for at in range(3))
    clip_factor = jnp.minimum(1.0, CLIP_RMS / jnp.sqrt(mean_square + EPSILON))
    clipped = clip_factor * outer_grad
    new_momentum = OUTER_MOMENTUM * momentum + clipped
    new_anchor = anchor - OUTER_RATE * (clipped + OUTER_MOMENTUM * new_momentum)
    new_inner = (MIX_KEEP * inner_float + (1.0 - MIX_KEEP) * new_anchor).astype(jnp.bfloat16)
    new_first = MIX_KEEP * adam_first[0] + (1.0 - MIX_KEEP) * first_mean
    new_second = MIX_KEEP * adam_second[0] + (1.0 - MIX_KEEP) * second_mean
    return (new_anchor, new_momentum, new_inner[None], new_first[None], new_second[None])


def solution(mesh):
    fine = Mesh(mesh.devices.reshape(SIZES), AXES)
    shared, own = P(FSDP, None), P(REP, FSDP, None)
    return jax.shard_map(
        per_device,
        mesh=fine,
        in_specs=(shared, own, shared, own, own),
        out_specs=(shared, shared, own, own, own),
        check_vma=False,
    )
```

```python
import jax
import jax.numpy as jnp
from jax import lax
from jax.sharding import Mesh, PartitionSpec as P

OUTER_MOMENTUM = 0.9
OUTER_RATE = 0.7
MIX_KEEP = 0.5
CLIP_RMS = 0.1
EPSILON = 1e-06

AXES = ("zs", "z1", "yh", "c", "yl", "x")
SIZES = (8, 2, 2, 2, 2, 4)
N_ZS, N_Z1, N_YH, N_C, N_YL, N_X = SIZES
REP = ("zs", "z1", "yh", "c")
NEAR = ("yh", "z1")
FSDP = ("yl", "x")
SWAP = ((0, 1), (1, 0))


def scatter_sum(parts, axis):
    return jnp.sum(lax.all_to_all(parts, axis, 0, 0), axis=0)


def gather_parts(part, axis, count):
    return lax.all_to_all(jnp.broadcast_to(part[None], (count,) + part.shape), axis, 0, 0)


def per_device(anchor, inner_weights, momentum, adam_first, adam_second):
    rows, columns = anchor.shape
    replica_count = N_ZS * N_Z1 * N_YH * N_C
    entries_total = rows * columns * N_YL * N_X
    inner_float = inner_weights[0].astype(jnp.float32)
    pseudo_grad = (anchor - inner_float).astype(jnp.bfloat16).astype(jnp.float32)
    block = (rows // (N_C * N_YH), columns // (N_Z1 * N_ZS))

    def split(array):
        array = array.reshape(N_C, N_YH, block[0], N_Z1 * N_ZS, block[1])
        return array.transpose(0, 1, 3, 2, 4).reshape((N_C, N_YH * N_Z1, N_ZS) + block)

    def join(blocks):
        blocks = blocks.reshape((N_C, N_YH, N_Z1 * N_ZS) + block)
        return blocks.transpose(0, 1, 3, 2, 4).reshape(rows, columns)

    first_core = lax.axis_index("c") == 0
    blocks = jnp.stack([split(pseudo_grad), split(adam_first[0]), split(adam_second[0])], axis=3)
    away = jnp.where(first_core, blocks[1], blocks[0])
    kept = jnp.where(first_core, blocks[0], blocks[1])
    terms = kept + lax.ppermute(away, "c", SWAP)
    terms = scatter_sum(terms, NEAR)
    mean = scatter_sum(terms, "zs") / replica_count

    spread = gather_parts(mean, "zs", N_ZS)
    half = gather_parts(spread, NEAR, N_YH * N_Z1)
    own_grad = half[:, :, 0]
    squares = jnp.sum(jnp.sum((own_grad * own_grad).reshape(-1, 8, 128), axis=0), axis=0, keepdims=True)
    parts = jnp.broadcast_to(squares[None], (N_C * N_YL * N_X, 1, 128))
    parts, half = lax.optimization_barrier((parts, half))
    sums = lax.all_to_all(parts, ("c",) + FSDP, 0, 0)
    other = lax.ppermute(half, "c", SWAP)

    both = jnp.stack([jnp.where(first_core, half, other), jnp.where(first_core, other, half)])
    outer_grad, first_mean, second_mean = (join(both[:, :, :, at]) for at in range(3))
    new_first = MIX_KEEP * adam_first[0] + (1.0 - MIX_KEEP) * first_mean
    new_second = MIX_KEEP * adam_second[0] + (1.0 - MIX_KEEP) * second_mean
    sums, new_first, new_second = lax.optimization_barrier((sums, new_first, new_second))
    mean_square = jnp.sum(sums) / entries_total
    clip_factor = jnp.minimum(1.0, CLIP_RMS / jnp.sqrt(mean_square + EPSILON))
    clipped = clip_factor * outer_grad
    new_momentum = OUTER_MOMENTUM * momentum + clipped
    new_anchor = anchor - OUTER_RATE * (clipped + OUTER_MOMENTUM * new_momentum)
    new_inner = (MIX_KEEP * inner_float + (1.0 - MIX_KEEP) * new_anchor).astype(jnp.bfloat16)
    return (new_anchor, new_momentum, new_inner[None], new_first[None], new_second[None])


def solution(mesh):
    fine = Mesh(mesh.devices.reshape(SIZES), AXES)
    shared, own = P(FSDP, None), P(REP, FSDP, None)
    return jax.shard_map(
        per_device,
        mesh=fine,
        in_specs=(shared, own, shared, own, own),
        out_specs=(shared, shared, own, own, own),
        check_vma=False,
    )
```

```python
import jax
import jax.numpy as jnp
from jax import lax
from jax.sharding import Mesh, PartitionSpec as P

OUTER_MOMENTUM = 0.9
OUTER_RATE = 0.7
MIX_KEEP = 0.5
CLIP_RMS = 0.1
EPSILON = 1e-06

AXES = ("zs", "z1", "yh", "c", "yl", "x")
SIZES = (8, 2, 2, 2, 2, 4)
N_ZS, N_Z1, N_YH, N_C, N_YL, N_X = SIZES
REP = ("zs", "z1", "yh", "c")
NEAR = ("yh", "z1")
FSDP = ("yl", "x")
SWAP = ((0, 1), (1, 0))


def scatter_sum(parts, axis):
    return jnp.sum(lax.all_to_all(parts, axis, 0, 0), axis=0)


def gather_parts(part, axis, count):
    return lax.all_to_all(jnp.broadcast_to(part[None], (count,) + part.shape), axis, 0, 0)


def per_device(anchor, inner_weights, momentum, adam_first, adam_second):
    rows, columns = anchor.shape
    replica_count = N_ZS * N_Z1 * N_YH * N_C
    entries_total = rows * columns * N_YL * N_X
    inner_float = inner_weights[0].astype(jnp.float32)
    pseudo_grad = (anchor - inner_float).astype(jnp.bfloat16).astype(jnp.float32)
    block = (rows // (N_C * N_YH), columns // (N_Z1 * N_ZS))

    def split(array):
        array = array.reshape(N_C, N_YH, block[0], N_Z1 * N_ZS, block[1])
        return array.transpose(0, 1, 3, 2, 4).reshape((N_C, N_YH * N_Z1, N_ZS) + block)

    def join(blocks):
        blocks = blocks.reshape((N_C, N_YH, N_Z1 * N_ZS) + block)
        return blocks.transpose(0, 1, 3, 2, 4).reshape(rows, columns)

    first_core = lax.axis_index("c") == 0
    blocks = jnp.stack([split(pseudo_grad), split(adam_first[0]), split(adam_second[0])], axis=3)
    away = jnp.where(first_core, blocks[1], blocks[0])
    kept = jnp.where(first_core, blocks[0], blocks[1])
    terms = kept + lax.ppermute(away, "c", SWAP)
    terms = scatter_sum(terms, NEAR)
    mean = scatter_sum(terms, "zs") / replica_count

    spread = gather_parts(mean, "zs", N_ZS)
    half = gather_parts(spread, NEAR, N_YH * N_Z1)
    own_grad = half[:, :, 0]
    squares = jnp.sum(jnp.sum((own_grad * own_grad).reshape(-1, 8, 128), axis=0), axis=0, keepdims=True)
    parts = jnp.broadcast_to(squares[None], (N_C * N_YL * N_X, 1, 128))
    parts, half = lax.optimization_barrier((parts, half))
    sums = lax.all_to_all(parts, ("c",) + FSDP, 0, 0)
    near_half = N_YH * N_Z1 // 2
    lower = lax.all_gather(half[:near_half], "c", axis=0)
    upper = lax.all_gather(half[near_half:], "c", axis=0)
    both = jnp.concatenate([lower, upper], axis=1)
    first_mean, second_mean = join(both[:, :, :, 1]), join(both[:, :, :, 2])
    new_first = MIX_KEEP * adam_first[0] + (1.0 - MIX_KEEP) * first_mean
    new_second = MIX_KEEP * adam_second[0] + (1.0 - MIX_KEEP) * second_mean
    sums, new_first, new_second = lax.optimization_barrier((sums, new_first, new_second))
    lanes = jnp.sum(sums, axis=0)
    total = jnp.dot(lanes, jnp.ones((lanes.shape[1], block[1]), jnp.float32), precision=lax.Precision.HIGHEST)
    mean_square = total[0] / entries_total
    clip_factor = jnp.minimum(1.0, CLIP_RMS / jnp.sqrt(mean_square + EPSILON))
    clipped = join(clip_factor * both[:, :, :, 0])
    new_momentum = OUTER_MOMENTUM * momentum + clipped
    new_anchor = anchor - OUTER_RATE * (clipped + OUTER_MOMENTUM * new_momentum)
    new_inner = (MIX_KEEP * inner_float + (1.0 - MIX_KEEP) * new_anchor).astype(jnp.bfloat16)
    return (new_anchor, new_momentum, new_inner[None], new_first[None], new_second[None])


def solution(mesh):
    fine = Mesh(mesh.devices.reshape(SIZES), AXES)
    shared, own = P(FSDP, None), P(REP, FSDP, None)
    return jax.shard_map(
        per_device,
        mesh=fine,
        in_specs=(shared, own, shared, own, own),
        out_specs=(shared, shared, own, own, own),
        check_vma=False,
    )
```

```python
import jax
import jax.numpy as jnp
from jax import lax
from jax.sharding import Mesh, PartitionSpec as P

OUTER_MOMENTUM = 0.9
OUTER_RATE = 0.7
MIX_KEEP = 0.5
CLIP_RMS = 0.1
EPSILON = 1e-06

AXES = ("zs", "z1", "yh", "c", "yl", "x")
SIZES = (8, 2, 2, 2, 2, 4)
N_ZS, N_Z1, N_YH, N_C, N_YL, N_X = SIZES
REP = ("zs", "z1", "yh", "c")
NEAR = ("yh", "z1")
FSDP = ("yl", "x")
SWAP = ((0, 1), (1, 0))


def scatter_sum(parts, axis):
    return jnp.sum(lax.all_to_all(parts, axis, 0, 0), axis=0)


def gather_parts(part, axis, count):
    return lax.all_to_all(jnp.broadcast_to(part[None], (count,) + part.shape), axis, 0, 0)


def per_device(anchor, inner_weights, momentum, adam_first, adam_second):
    rows, columns = anchor.shape
    replica_count = N_ZS * N_Z1 * N_YH * N_C
    entries_total = rows * columns * N_YL * N_X
    inner_float = inner_weights[0].astype(jnp.float32)
    pseudo_grad = anchor - inner_float
    block = (rows // (N_C * N_YH), columns // (N_Z1 * N_ZS))

    def split(array):
        array = array.reshape(N_C, N_YH, block[0], N_Z1 * N_ZS, block[1])
        return array.transpose(0, 1, 3, 2, 4).reshape((N_C, N_YH * N_Z1, N_ZS) + block)

    def join(blocks):
        blocks = blocks.reshape((N_C, N_YH, N_Z1 * N_ZS) + block)
        return blocks.transpose(0, 1, 3, 2, 4).reshape(rows, columns)

    first_core = lax.axis_index("c") == 0
    blocks = jnp.stack([split(pseudo_grad), split(adam_first[0]), split(adam_second[0])], axis=3)
    away = jnp.where(first_core, blocks[1], blocks[0])
    kept = jnp.where(first_core, blocks[0], blocks[1])
    terms = kept + lax.ppermute(away, "c", SWAP)
    terms = scatter_sum(terms, NEAR)
    mean = scatter_sum(terms, "zs") / replica_count

    spread = gather_parts(mean, "zs", N_ZS)
    half = gather_parts(spread, NEAR, N_YH * N_Z1)
    own_grad = half[:, :, 0]
    squares = jnp.sum(jnp.sum((own_grad * own_grad).reshape(-1, 8, 128), axis=0), axis=0, keepdims=True)
    parts = jnp.broadcast_to(squares[None], (N_C * N_YL * N_X, 1, 128))
    parts, half = lax.optimization_barrier((parts, half))
    sums = lax.all_to_all(parts, ("c",) + FSDP, 0, 0)
    near_half = N_YH * N_Z1 // 2
    lower = lax.all_gather(half[:near_half], "c", axis=0)
    upper = lax.all_gather(half[near_half:], "c", axis=0)
    both = jnp.concatenate([lower, upper], axis=1)
    first_mean, second_mean = join(both[:, :, :, 1]), join(both[:, :, :, 2])
    new_first = MIX_KEEP * adam_first[0] + (1.0 - MIX_KEEP) * first_mean
    new_second = MIX_KEEP * adam_second[0] + (1.0 - MIX_KEEP) * second_mean
    sums, new_first, new_second = lax.optimization_barrier((sums, new_first, new_second))
    lanes = jnp.sum(sums, axis=0)
    total = jnp.dot(lanes, jnp.ones((lanes.shape[1], block[1]), jnp.float32), precision=lax.Precision.HIGHEST)
    mean_square = total[0] / entries_total
    clip_factor = jnp.minimum(1.0, CLIP_RMS / jnp.sqrt(mean_square + EPSILON))
    clipped = join(clip_factor * both[:, :, :, 0])
    new_momentum = OUTER_MOMENTUM * momentum + clipped
    new_anchor = anchor - OUTER_RATE * (clipped + OUTER_MOMENTUM * new_momentum)
    new_inner = (MIX_KEEP * inner_float + (1.0 - MIX_KEEP) * new_anchor).astype(jnp.bfloat16)
    return (new_anchor, new_momentum, new_inner[None], new_first[None], new_second[None])


def solution(mesh):
    fine = Mesh(mesh.devices.reshape(SIZES), AXES)
    shared, own = P(FSDP, None), P(REP, FSDP, None)
    return jax.shard_map(
        per_device,
        mesh=fine,
        in_specs=(shared, own, shared, own, own),
        out_specs=(shared, shared, own, own, own),
        check_vma=False,
    )
```

```python
import jax
import jax.numpy as jnp
from jax import lax
from jax.sharding import Mesh, PartitionSpec as P

OUTER_MOMENTUM = 0.9
OUTER_RATE = 0.7
MIX_KEEP = 0.5
CLIP_RMS = 0.1
EPSILON = 1e-06

AXES = ("zs", "z1", "yh", "c", "yl", "x")
SIZES = (8, 2, 2, 2, 2, 4)
N_ZS, N_Z1, N_YH, N_C, N_YL, N_X = SIZES
REP = ("zs", "z1", "yh", "c")
NEAR = ("z1", "yh")
FSDP = ("yl", "x")
SWAP = ((0, 1), (1, 0))


def scatter_sum(parts, axis):
    return jnp.sum(lax.all_to_all(parts, axis, 0, 0), axis=0)


def gather_parts(part, axis, count):
    return lax.all_to_all(jnp.broadcast_to(part[None], (count,) + part.shape), axis, 0, 0)


def per_device(anchor, inner_weights, momentum, adam_first, adam_second):
    rows, columns = anchor.shape
    replica_count = N_ZS * N_Z1 * N_YH * N_C
    entries_total = rows * columns * N_YL * N_X
    inner_float = inner_weights[0].astype(jnp.float32)
    pseudo_grad = anchor - inner_float
    block = (rows // (N_C * N_Z1), columns // (N_YH * N_ZS))

    def split(array):
        array = array.reshape(N_C, N_Z1, block[0], N_YH * N_ZS, block[1])
        return array.transpose(0, 1, 3, 2, 4).reshape((N_C, N_Z1 * N_YH, N_ZS) + block)

    def join(blocks):
        blocks = blocks.reshape((N_C, N_Z1, N_YH * N_ZS) + block)
        return blocks.transpose(0, 1, 3, 2, 4).reshape(rows, columns)

    first_core = lax.axis_index("c") == 0
    blocks = jnp.stack([split(pseudo_grad), split(adam_first[0]), split(adam_second[0])], axis=3)
    away = jnp.where(first_core, blocks[1], blocks[0])
    kept = jnp.where(first_core, blocks[0], blocks[1])
    terms = kept + lax.ppermute(away, "c", SWAP)
    terms = scatter_sum(terms, NEAR)
    mean = scatter_sum(terms, "zs") / replica_count

    spread = gather_parts(mean, "zs", N_ZS)
    half = gather_parts(spread, NEAR, N_Z1 * N_YH)
    own_grad = half[:, :, 0]
    squares = jnp.sum(jnp.sum((own_grad * own_grad).reshape(-1, 8, 128), axis=0), axis=0, keepdims=True)
    parts = jnp.broadcast_to(squares[None], (N_C * N_YL * N_X, 1, 128))
    parts, half = lax.optimization_barrier((parts, half))
    sums = lax.all_to_all(parts, ("c",) + FSDP, 0, 0)
    near_half = N_Z1 * N_YH // 2
    lower = lax.all_gather(half[:near_half], "c", axis=0)
    upper = lax.all_gather(half[near_half:], "c", axis=0)
    both = jnp.concatenate([lower, upper], axis=1)
    first_mean, second_mean = join(both[:, :, :, 1]), join(both[:, :, :, 2])
    new_first = MIX_KEEP * adam_first[0] + (1.0 - MIX_KEEP) * first_mean
    new_second = MIX_KEEP * adam_second[0] + (1.0 - MIX_KEEP) * second_mean
    sums, new_first, new_second = lax.optimization_barrier((sums, new_first, new_second))
    lanes = jnp.sum(sums, axis=0)
    total = jnp.dot(lanes, jnp.ones((lanes.shape[1], block[1]), jnp.float32), precision=lax.Precision.HIGHEST)
    mean_square = total[0] / entries_total
    clip_factor = jnp.minimum(1.0, CLIP_RMS / jnp.sqrt(mean_square + EPSILON))
    clipped = join(clip_factor * both[:, :, :, 0])
    new_momentum = OUTER_MOMENTUM * momentum + clipped
    new_anchor = anchor - OUTER_RATE * (clipped + OUTER_MOMENTUM * new_momentum)
    new_inner = (MIX_KEEP * inner_float + (1.0 - MIX_KEEP) * new_anchor).astype(jnp.bfloat16)
    return (new_anchor, new_momentum, new_inner[None], new_first[None], new_second[None])


def solution(mesh):
    fine = Mesh(mesh.devices.reshape(SIZES), AXES)
    shared, own = P(FSDP, None), P(REP, FSDP, None)
    return jax.shard_map(
        per_device,
        mesh=fine,
        in_specs=(shared, own, shared, own, own),
        out_specs=(shared, shared, own, own, own),
        check_vma=False,
    )
```

```python
import jax
import jax.numpy as jnp
from jax import lax
from jax.sharding import Mesh, PartitionSpec as P

OUTER_MOMENTUM = 0.9
OUTER_RATE = 0.7
MIX_KEEP = 0.5
CLIP_RMS = 0.1
EPSILON = 1e-06

AXES = ("zs", "z1", "yh", "c", "yl", "x")
SIZES = (8, 2, 2, 2, 2, 4)
N_ZS, N_Z1, N_YH, N_C, N_YL, N_X = SIZES
REP = ("zs", "z1", "yh", "c")
NEAR = ("z1", "yh")
FSDP = ("yl", "x")
SWAP = ((0, 1), (1, 0))


def scatter_sum(parts, axis):
    return jnp.sum(lax.all_to_all(parts, axis, 0, 0), axis=0)


def gather_parts(part, axis, count):
    return lax.all_to_all(jnp.broadcast_to(part[None], (count,) + part.shape), axis, 0, 0)


def per_device(anchor, inner_weights, momentum, adam_first, adam_second):
    rows, columns = anchor.shape
    replica_count = N_ZS * N_Z1 * N_YH * N_C
    entries_total = rows * columns * N_YL * N_X
    inner_float = inner_weights[0].astype(jnp.float32)
    pseudo_grad = anchor - inner_float
    block = (rows // (N_C * N_Z1), columns // (N_YH * N_ZS))

    def split(array):
        array = array.reshape(N_C, N_Z1, block[0], N_YH * N_ZS, block[1])
        return array.transpose(0, 1, 3, 2, 4).reshape((N_C, N_Z1 * N_YH, N_ZS) + block)

    def join(blocks):
        blocks = blocks.reshape((N_C, N_Z1, N_YH * N_ZS) + block)
        return blocks.transpose(0, 1, 3, 2, 4).reshape(rows, columns)

    first_core = lax.axis_index("c") == 0
    blocks = jnp.stack([split(pseudo_grad), split(adam_first[0]), split(adam_second[0])], axis=3)
    away = jnp.where(first_core, blocks[1], blocks[0])
    kept = jnp.where(first_core, blocks[0], blocks[1])
    received, kept_momentum = lax.optimization_barrier((lax.ppermute(away, "c", SWAP), OUTER_MOMENTUM * momentum))
    terms = kept + received
    terms = scatter_sum(terms, NEAR)
    mean = scatter_sum(terms, "zs") / replica_count

    spread = gather_parts(mean, "zs", N_ZS)
    half = gather_parts(spread, NEAR, N_Z1 * N_YH)
    own_grad = half[:, :, 0]
    squares = jnp.sum(jnp.sum((own_grad * own_grad).reshape(-1, 8, 128), axis=0), axis=0, keepdims=True)
    parts = jnp.broadcast_to(squares[None], (N_C * N_YL * N_X, 1, 128))
    parts, half = lax.optimization_barrier((parts, half))
    sums = lax.all_to_all(parts, ("c",) + FSDP, 0, 0)
    near_half = N_Z1 * N_YH // 2
    lower = lax.all_gather(half[:near_half], "c", axis=0)
    upper = lax.all_gather(half[near_half:], "c", axis=0)
    both = jnp.concatenate([lower, upper], axis=1)
    first_mean, second_mean = join(both[:, :, :, 1]), join(both[:, :, :, 2])
    new_first = MIX_KEEP * adam_first[0] + (1.0 - MIX_KEEP) * first_mean
    new_second = MIX_KEEP * adam_second[0] + (1.0 - MIX_KEEP) * second_mean
    sums, new_first, new_second = lax.optimization_barrier((sums, new_first, new_second))
    lanes = jnp.sum(sums, axis=0)
    total = jnp.dot(lanes, jnp.ones((lanes.shape[1], block[1]), jnp.float32), precision=lax.Precision.HIGHEST)
    mean_square = total[0] / entries_total
    clip_factor = jnp.minimum(1.0, CLIP_RMS / jnp.sqrt(mean_square + EPSILON))
    clipped = join(clip_factor * both[:, :, :, 0])
    new_momentum = kept_momentum + clipped
    new_anchor = anchor - OUTER_RATE * (clipped + OUTER_MOMENTUM * new_momentum)
    new_inner = (MIX_KEEP * inner_float + (1.0 - MIX_KEEP) * new_anchor).astype(jnp.bfloat16)
    return (new_anchor, new_momentum, new_inner[None], new_first[None], new_second[None])


def solution(mesh):
    fine = Mesh(mesh.devices.reshape(SIZES), AXES)
    shared, own = P(FSDP, None), P(REP, FSDP, None)
    return jax.shard_map(
        per_device,
        mesh=fine,
        in_specs=(shared, own, shared, own, own),
        out_specs=(shared, shared, own, own, own),
        check_vma=False,
    )
```
